256 devices in a mesh: rows: 128 (over z, y, x), out: 2 (over core).
Axes of the slice: x: 4, y: 4, z: 8, core: 2. Of those that a mesh axis runs over, the one named last changes fastest.
Arguments:
- features: float32 [131072, 256], P('rows'), may hold values from -8 to 8
- targets: float32 [131072, 512], P('rows', 'out'), may hold values from -6 to 6
- nugget: float32 [131072], P('rows'), may hold values from 0.3 to 1.5
- pattern: int32 [128, 5], P('rows'), may hold values from 0 to 1, as said below
Outputs:
- solution: float32 [131072, 512], P('rows', 'out')
- residual: float32 [131072, 512], P('rows', 'out')
- image: float32 [131072, 512], P('rows', 'out')
The draws below stay inside these ranges and needn't reach their ends.
Inputs may be any that keep to these rules, and one draw needn't show every extreme that they name: pattern[i, 2 + o] = 1 marks a stored tile of row block i and column block i + o. The pattern is symmetric (pattern[i, 2 + o] = pattern[i + o, 2 - o]), every entry of column 2 is 1, entries whose column block falls outside 0 to 127 are 0, some row block holds all 5 tiles, and row block 127 holds its tiles with the 2 row blocks below it.
All inputs are finite; a program needn't handle non-finite values.
Results may differ from the reference program's by a relative error of at most 0.013.
Values may be sent and summed in bfloat16 or wider, within the bound.
A program may use at most 64 MiB of HBM per device.

```python
import math
import jax
import jax.numpy as jnp
from jax import lax

TILE = 1024
D = 256
OUTS = 512
W = 2
ITERS = 2
NB = 128
N = 131072


def latent_pair(key):
    key_gauss = jax.random.fold_in(key, 0)
    gauss = jnp.clip(jax.random.normal(key_gauss, (N, 8), jnp.float32), -4.5, 4.5)
    return gauss


def draw_features(key, part):
    gauss = latent_pair(key)
    key = jax.random.fold_in(key, 5)
    key_gain, key_noise = jax.random.split(key)
    gains = jax.random.uniform(key_gain, (1, D), jnp.float32, 0.8, 1.2)
    latent = 0.6 * gauss
    noise = 0.35 * jnp.clip(jax.random.normal(key_noise, (N, D), jnp.float32), -5.0, 5.0)
    spread = jnp.tile(latent, (1, D // 8))
    return jnp.clip(spread * gains + noise, -8.0, 8.0)


def draw_targets(key, part):
    gauss = latent_pair(key)
    key = jax.random.fold_in(key, 7)
    key_amp, key_sign, key_noise = jax.random.split(key, 3)
    latent = 0.6 * gauss
    noise = 0.5 * jax.random.normal(key_noise, (N, OUTS), jnp.float32)
    amplitude = jnp.exp(jax.random.uniform(key_amp, (1, OUTS), jnp.float32, math.log(0.5), math.log(1.5)))
    signs = jnp.where(jax.random.randint(key_sign, (1, OUTS), 0, 2) == 0, -1.0, 1.0)
    shape_part = jnp.exp(0.4 * (latent[:, 0:1] + latent[:, 1:2]))
    common = 2.0 * signs * amplitude * shape_part
    return jnp.clip(common + noise, -6.0, 6.0)


def draw_pattern(key, part):
    key = jax.random.fold_in(key, 11)
    key_level, key_bits = jax.random.split(key)
    level = jax.random.randint(key_level, (NB, 1), 1, 4)
    bits = jax.random.randint(key_bits, (NB, W), 0, 4) < level
    index = jnp.arange(NB, dtype=jnp.int32)[:, None]
    offsets = jnp.arange(1, W + 1, dtype=jnp.int32)[None, :]
    inside = index + offsets < NB
    middle = NB // 2
    forced = (index == middle) | (index + offsets == middle) | (index + offsets == NB - 1)
    upper = ((bits | forced) & inside).astype(jnp.int32)
    rows = jnp.arange(NB, dtype=jnp.int32)
    lower_cols = []
    for offset in range(1, W + 1):
        lower_cols.append(jnp.roll(upper[:, offset - 1], offset) * (rows >= offset).astype(jnp.int32))
    lower = jnp.stack(lower_cols, axis=1)
    centre = jnp.ones((NB, 1), jnp.int32)
    return jnp.concatenate([lower[:, ::-1], centre, upper], axis=1)


def steps_of(stream_key, extent, pieces, least, high):
    def one(position, blocks):
        heights = jax.random.uniform(jax.random.fold_in(jax.random.fold_in(stream_key, 6), position), (blocks,), jnp.float32, least / len(pieces), high / len(pieces))
        return jnp.repeat(jnp.exp(heights), extent[position] // blocks).reshape((-1,) + (1,) * (len(extent) - position - 1))

    level = one(*pieces[0])
    for cut in pieces[1:]:
        level = level * one(*cut)
    return level


def setup_inputs(seed: int = 0) -> dict:
    key_list = jax.random.split(jax.random.key(seed), 5)
    return {
        "features": draw_features(jax.random.fold_in(key_list[4], 71), 0),
        "targets": draw_targets(jax.random.fold_in(key_list[4], 71), 0),
        "nugget": jnp.clip(jnp.exp(math.log(1.5) - 1.60943787 * jax.random.uniform(key_list[2], (N,), jnp.float32) ** steps_of(key_list[2], (N,), ((0, 128),), -0.2, 0.2)), 0.3, 1.5),
        "pattern": draw_pattern(jax.random.fold_in(key_list[4], 71), 0),
    }


def wendland(rows_a, rows_b):
    norms_a = lax.optimization_barrier(jnp.sum(rows_a * rows_a, axis=1))
    norms_b = lax.optimization_barrier(jnp.sum(rows_b * rows_b, axis=1))
    cross = jnp.dot(rows_a, rows_b.T, precision=lax.Precision.HIGHEST, preferred_element_type=jnp.float32)
    dist_sq = jnp.maximum(norms_a[:, None] + norms_b[None, :] - 2.0 * cross, 0.0)
    radius = 1.25 * math.sqrt(2.0 * rows_a.shape[1])
    ratio = jnp.sqrt(dist_sq) / radius
    falloff = jnp.maximum(1.0 - ratio, 0.0)
    return falloff ** 4 * (4.0 * ratio + 1.0)

def reference(features, targets, nugget, pattern):
    feature_blocks = features.reshape(NB, TILE, D)
    pattern_f = pattern.astype(jnp.float32)
    block_ids = jnp.arange(NB, dtype=jnp.int32)

    def masked_tile(index, offset):
        other = jnp.clip(index + offset, 0, NB - 1).astype(jnp.int32)
        return (other, pattern_f[index, W + offset] * wendland(feature_blocks[index], feature_blocks[other]))

    def row_sums(index):
        summed = jnp.zeros((TILE,), jnp.float32)
        for offset in range(-W, W + 1):
            other, kernel = masked_tile(index, offset)
            summed = summed + lax.optimization_barrier(jnp.sum(kernel, axis=1))
        return summed
    totals = lax.map(row_sums, block_ids).reshape(N)

    def operate(field):
        field16 = field.astype(jnp.bfloat16).reshape(NB, TILE, OUTS)

        def one_block(index):
            summed = jnp.zeros((TILE, OUTS), jnp.float32)
            for offset in range(-W, W + 1):
                other, kernel = masked_tile(index, offset)
                summed = summed + jnp.dot(kernel.astype(jnp.bfloat16), field16[other], preferred_element_type=jnp.float32)
            return summed
        products = lax.map(one_block, block_ids).reshape(N, OUTS)
        return nugget[:, None] * field + (totals[:, None] * field + products) / TILE
    solution = jnp.zeros_like(targets)
    residual = targets
    image = operate(residual)
    image_step = jnp.zeros_like(targets)
    search_image = jnp.zeros_like(targets)
    direction = jnp.zeros_like(targets)
    norm_prev = jnp.ones((OUTS,), jnp.float32)
    step_prev = jnp.ones((OUTS,), jnp.float32)
    for step in range(ITERS):
        norm_sq = lax.optimization_barrier(jnp.sum(residual * residual, axis=0))
        cross_term = lax.optimization_barrier(jnp.sum(image * residual, axis=0))
        product = operate(image)
        if step == 0:
            momentum = jnp.zeros((OUTS,), jnp.float32)
            step_len = norm_sq / cross_term
        else:
            momentum = norm_sq / norm_prev
            step_len = norm_sq / (cross_term - momentum * norm_sq / step_prev)
        image_step = product + momentum * image_step
        search_image = image + momentum * search_image
        direction = residual + momentum * direction
        solution = solution + step_len * direction
        residual = residual - step_len * search_image
        image = image - step_len * image_step
        norm_prev = norm_sq
        step_prev = step_len
    return (solution, residual, image)
```

```python
import functools
import math

import jax
import jax.numpy as jnp
from jax import lax
from jax.experimental import pallas as pl
from jax.experimental.pallas import tpu as pltpu
from jax.sharding import PartitionSpec as P

MESH = pl.DeviceIdType.MESH
F32, BF16 = jnp.float32, jnp.bfloat16
NT = (((1,), (1,)), ((), ()))
X, Y, Z = 4, 4, 8
NB = X * Y * Z
T = 1024
D = 256
G = 128
H = T // 2
RADIUS = 1.25 * math.sqrt(2.0 * D) / math.sqrt(2.0)
M2, M1, P1, P2 = range(4)
TILE_OF = (0, 1, 3, 4)
COPIES = (
    (None, 1, 1, M1),
    (None, 0, -1, P1),
    (None, 0, 1, M1),
    (None, 1, -1, P1),
    (M1, 1, 1, M2),
    (P1, 0, -1, P2),
    (P2, 0, Y, M2),
    (M2, 1, -Y, P2),
)


def kernel(
    f_hbm, t_hbm, n_ref, pat_ref, sol_hbm, res_hbm, img_hbm,
    f32, t32, f16, fn, na, ktile, diag, x16, nb, cur, w1s, w2s, r1s, obuf, coef, xb, yb, zb,
    in_sem, out_sem, f_send, f_recv, sib_send, sib_recv, e_send, e_recv, ar_send, ar_recv,
):
    r, c = lax.axis_index("rows"), lax.axis_index("out")
    x, y, z = lax.rem(r, X), lax.rem(r // X, Y), r // (X * Y)

    def at(step):
        return (lax.rem(r + step + NB, NB), c)

    def along(axis, d):
        if axis == 0:
            return ((z * Y + y) * X + lax.rem(x + d, X), c)
        if axis == 1:
            return ((z * Y + lax.rem(y + d, Y)) * X + x, c)
        return ((lax.rem(z + d, Z) * Y + y) * X + x, c)

    sibling = (r, 1 - c)
    load_f = pltpu.make_async_copy(f_hbm, f32, in_sem.at[0])
    load_t = pltpu.make_async_copy(t_hbm, t32, in_sem.at[1])
    load_f.start()
    load_t.start()

    barrier = pltpu.get_barrier_semaphore()
    peers = [at(1), at(-1), at(Y), at(-Y), sibling]
    for axis, size in enumerate((X, Y, Z)):
        peers += [along(axis, d) for d in range(1, size)]
    for peer in peers:
        pl.semaphore_signal(barrier, inc=1, device_id=peer, device_id_type=MESH)

    def feature_rows(half):
        return pl.ds(pl.multiple_of(c * H + half * (H // 2), H // 2), H // 2)

    def f_copy(i):
        src, half, to, dst = COPIES[i]
        rows = feature_rows(half)
        return pltpu.make_async_remote_copy(
            src_ref=f16.at[rows] if src is None else fn.at[src, rows],
            dst_ref=fn.at[dst, rows],
            send_sem=f_send.at[i], recv_sem=f_recv.at[i],
            device_id=at(to), device_id_type=MESH,
        )

    def s_copy(slot):
        rows = pl.ds(pl.multiple_of(c * H, H), H)
        return pltpu.make_async_remote_copy(
            src_ref=fn.at[slot, rows], dst_ref=fn.at[slot, rows],
            send_sem=sib_send.at[slot], recv_sem=sib_recv.at[slot],
            device_id=sibling, device_id_type=MESH,
        )

    def e_copy(s, i):
        src, half, to, dst = COPIES[i]
        rows = pl.ds(half * H, H)
        return pltpu.make_async_remote_copy(
            src_ref=x16.at[s, rows] if src is None else nb.at[s, src, rows],
            dst_ref=nb.at[s, dst, rows],
            send_sem=e_send.at[s, i], recv_sem=e_recv.at[s, i],
            device_id=at(to), device_id_type=MESH,
        )

    def ar_buf(axis, k):
        return ((xb, x), (yb, y), (zb, z))[axis]

    def ar_copies(k, axis):
        buf, own = ar_buf(axis, k)
        first = (0, X - 1, X + Y - 2)[axis]
        return [
            pltpu.make_async_remote_copy(
                src_ref=buf.at[k, own], dst_ref=buf.at[k, own],
                send_sem=ar_send.at[k, first + d - 1], recv_sem=ar_recv.at[k, first + d - 1],
                device_id=along(axis, d), device_id_type=MESH,
            )
            for d in range(1, (X, Y, Z)[axis])
        ]

    def ar_start(k, axis, value):
        buf, own = ar_buf(axis, k)
        buf[k, own] = value
        for copy in ar_copies(k, axis):
            copy.start()

    def ar_finish(k, axis):
        for copy in ar_copies(k, axis):
            copy.wait_recv()
        buf, _ = ar_buf(axis, k)
        total = buf[k, 0]
        for i in range(1, (X, Y, Z)[axis]):
            total = total + buf[k, i]
        return total

    load_f.wait()
    f16[...] = f32[...].astype(BF16)
    pl.semaphore_wait(barrier, len(peers))
    for i in range(4):
        f_copy(i).start()
    load_t.wait()
    for g in range(2):
        x16[g] = t32[:, g * G:(g + 1) * G].astype(BF16)
        cur[g] = t32[:, g * G:(g + 1) * G]
        for i in range(4):
            e_copy(g, i).start()

    def squares(block):
        wide = block.astype(F32)
        sq = wide * wide
        high = sq.astype(BF16)
        return high, (sq - high.astype(F32)).astype(BF16)

    halves_col = jnp.full((D, G), 0.5, BF16)
    halves_row = jnp.full((16, D), 0.5, BF16)
    high, low = squares(f16[...])
    na[...] = jnp.dot(high, halves_col, preferred_element_type=F32) + jnp.dot(
        low, halves_col, preferred_element_type=F32
    )
    diag[...] = jnp.zeros_like(diag)

    def build(tile, other):
        high, low = squares(other[...])
        norms = lax.dot_general(halves_row, high, NT, preferred_element_type=F32) + lax.dot_general(
            halves_row, low, NT, preferred_element_type=F32
        )
        kept = pat_ref[0, tile].astype(F32)
        base = kept * (1.0 / (RADIUS**4 * T))
        slope = kept * (4.0 / (RADIUS**5 * T))

        def chunk(i, _):
            rows = pl.ds(pl.multiple_of(i * H, H), H)
            cross = lax.dot_general(f16[rows, :], other[...], NT, preferred_element_type=F32)
            norm = na[rows, :]
            summed = diag[rows, :]
            for lane in range(T // G):
                cols = slice(lane * G, (lane + 1) * G)
                half_sq = jnp.maximum(norm + norms[0:1, cols] - cross[:, cols], 1e-30)
                dist = half_sq * lax.rsqrt(half_sq)
                fall = jnp.maximum(RADIUS - dist, 0.0)
                fall = fall * fall
                value = (fall * fall) * (dist * slope + base)
                ktile[tile, rows, cols] = value.astype(BF16)
                summed = summed + value
            diag[rows, :] = summed
            return 0

        lax.fori_loop(0, T // H, chunk, 0)

    build(2, f16)
    f_copy(0).wait_recv()
    f_copy(4).start()
    f_copy(1).wait_recv()
    f_copy(5).start()
    f_copy(2).wait_recv()
    s_copy(M1).start()
    f_copy(3).wait_recv()
    s_copy(P1).start()
    s_copy(M1).wait_recv()
    build(1, fn.at[M1])
    f_copy(4).wait_recv()
    f_copy(7).start()
    f_copy(5).wait_recv()
    f_copy(6).start()
    s_copy(P1).wait_recv()
    build(3, fn.at[P1])
    e_copy(0, 0).wait_recv()
    e_copy(0, 4).start()
    e_copy(0, 1).wait_recv()
    e_copy(0, 5).start()
    f_copy(6).wait_recv()
    s_copy(M2).start()
    f_copy(7).wait_recv()
    s_copy(P2).start()
    s_copy(M2).wait_recv()
    build(0, fn.at[M2])
    e_copy(0, 4).wait_recv()
    e_copy(0, 7).start()
    e_copy(0, 5).wait_recv()
    e_copy(0, 6).start()
    e_copy(1, 0).wait_recv()
    e_copy(1, 4).start()
    e_copy(1, 1).wait_recv()
    e_copy(1, 5).start()
    s_copy(P2).wait_recv()
    build(4, fn.at[P2])
    nugget = jnp.broadcast_to(n_ref[0:1, :], (G, T)).T
    diag[...] = nugget + jnp.sum(diag[...], axis=1, keepdims=True)

    def out_copy(g, i):
        cols = pl.ds(pl.multiple_of(g * G, G), G)
        out = (sol_hbm, res_hbm, img_hbm)[i]
        return pltpu.make_async_copy(obuf.at[g, i], out.at[:, cols], out_sem.at[g, i])

    def step(s, _):
        g, e = lax.rem(s, 2), s // 2
        cols = pl.ds(pl.multiple_of(g * G, G), G)

        @pl.when(s >= 1)
        def _():
            e_copy(s, 4).wait_recv()
            e_copy(s, 7).start()
            e_copy(s, 5).wait_recv()
            e_copy(s, 6).start()

        @pl.when((s >= 1) & (s <= 4))
        def _():
            ar_start(s - 1, 1, ar_finish(s - 1, 0))
            e_copy(s + 1, 0).wait_recv()
            e_copy(s + 1, 4).start()
            e_copy(s + 1, 1).wait_recv()
            e_copy(s + 1, 5).start()
            ar_start(s - 1, 2, ar_finish(s - 1, 1))

        @pl.when(e == 1)
        def _():
            total = ar_finish(s - 2, 2)
            norm, cross = total[0:1, :], total[1:2, :]
            coef[g, 0:1, :] = norm
            coef[g, 1:2, :] = norm / cross

        @pl.when(e == 2)
        def _():
            total = ar_finish(s - 2, 2)
            norm, cross = total[0:1, :], total[1:2, :]
            step0 = coef[g, 1:2, :]
            momentum = norm / coef[g, 0:1, :]
            step1 = norm / (cross - momentum * norm / step0)
            coef[g, 2:3, :] = momentum
            coef[g, 3:4, :] = step1
            start = t32[:, cols]
            res = r1s[g]
            obuf[g, 0] = step0 * start + step1 * (res + momentum * start)
            obuf[g, 1] = res - step1 * (cur[g] + momentum * w1s[g])
            out_copy(g, 0).start()
            out_copy(g, 1).start()

        for i in (2, 3, 6, 7):
            e_copy(s, i).wait_recv()

        def chunk(i, sums):
            rows = pl.ds(pl.multiple_of(i * H, H), H)
            acc = jnp.dot(ktile[2, rows, :], x16[s], preferred_element_type=F32)
            for slot in (M1, P1, M2, P2):
                acc = acc + jnp.dot(
                    ktile[TILE_OF[slot], rows, :], nb[s, slot], preferred_element_type=F32
                )
            w2s[g, rows] = acc + diag[rows, :] * cur[g, rows]
            return sums

        lax.fori_loop(0, 2, chunk, 0)

        def reduce_start(norm, cross):
            ar_start(s, 0, jnp.concatenate(
                [jnp.sum(norm, axis=0, keepdims=True), jnp.sum(cross, axis=0, keepdims=True),
                 jnp.zeros((6, G), F32)], axis=0))

        @pl.when(e == 0)
        def _():
            w = w2s[g]
            x16[s + 2] = w.astype(BF16)
            for i in range(4):
                e_copy(s + 2, i).start()
            start = t32[:, cols]
            cur[g] = w
            w1s[g] = w
            reduce_start(start * start, w * start)

        @pl.when(e == 1)
        def _():
            step0 = coef[g, 1:2, :]
            image = cur[g] - step0 * w2s[g]
            x16[s + 2] = image.astype(BF16)
            for i in range(4):
                e_copy(s + 2, i).start()
            cur[g] = image
            res = t32[:, cols] - step0 * w1s[g]
            r1s[g] = res
            obuf[g, 2] = w2s[g]
            reduce_start(res * res, image * res)

        @pl.when(e == 2)
        def _():
            momentum, step1 = coef[g, 2:3, :], coef[g, 3:4, :]
            obuf[g, 2] = cur[g] - step1 * (w2s[g] + momentum * obuf[g, 2])
            out_copy(g, 2).start()

        return 0

    lax.fori_loop(0, 6, step, 0)

    for i in range(8):
        f_copy(i).wait_send()
    for slot in range(4):
        s_copy(slot).wait_send()

    def drain(s, _):
        for i in range(8):
            e_copy(s, i).wait_send()

        @pl.when(s < 4)
        def _():
            for axis in range(3):
                for copy in ar_copies(s, axis):
                    copy.wait_send()

        @pl.when(s < 2)
        def _():
            for i in range(3):
                out_copy(s, i).wait()

        return 0

    lax.fori_loop(0, 6, drain, 0)


def body(features, targets, nugget, pattern):
    out = jax.ShapeDtypeStruct((T, 2 * G), F32)
    dma = pltpu.SemaphoreType.DMA
    return pl.pallas_call(
        kernel,
        out_shape=(out, out, out),
        in_specs=[
            pl.BlockSpec(memory_space=pl.ANY),
            pl.BlockSpec(memory_space=pl.ANY),
            pl.BlockSpec(memory_space=pltpu.VMEM),
            pl.BlockSpec(memory_space=pltpu.SMEM),
        ],
        out_specs=(pl.BlockSpec(memory_space=pl.ANY),) * 3,
        scratch_shapes=[
            pltpu.VMEM((T, D), F32),
            pltpu.VMEM((T, 2 * G), F32),
            pltpu.VMEM((T, D), BF16),
            pltpu.VMEM((4, T, D), BF16),
            pltpu.VMEM((T, G), F32),
            pltpu.VMEM((5, T, T), BF16),
            pltpu.VMEM((T, G), F32),
            pltpu.VMEM((6, T, G), BF16),
            pltpu.VMEM((6, 4, T, G), BF16),
            pltpu.VMEM((2, T, G), F32),
            pltpu.VMEM((2, T, G), F32),
            pltpu.VMEM((2, T, G), F32),
            pltpu.VMEM((2, T, G), F32),
            pltpu.VMEM((2, 3, T, G), F32),
            pltpu.VMEM((2, 8, G), F32),
            pltpu.VMEM((4, X, 8, G), F32),
            pltpu.VMEM((4, Y, 8, G), F32),
            pltpu.VMEM((4, Z, 8, G), F32),
            dma((2,)),
            dma((2, 3)),
            dma((8,)),
            dma((8,)),
            dma((4,)),
            dma((4,)),
            dma((6, 8)),
            dma((6, 8)),
            dma((4, X + Y + Z - 3)),
            dma((4, X + Y + Z - 3)),
        ],
        compiler_params=pltpu.CompilerParams(
            collective_id=0, has_side_effects=True, vmem_limit_bytes=56 * 2**20
        ),
        name="cascaded_cg",
    )(features, targets, nugget.reshape(1, T), pattern)


def solution(mesh):
    return jax.shard_map(
        body,
        mesh=mesh,
        in_specs=(P("rows", None), P("rows", "out"), P("rows"), P("rows", None)),
        out_specs=(P("rows", "out"), P("rows", "out"), P("rows", "out")),
        check_vma=False,
    )
```

```python
import functools
import math

import jax
import jax.numpy as jnp
from jax import lax
from jax.experimental import pallas as pl
from jax.experimental.pallas import tpu as pltpu
from jax.sharding import PartitionSpec as P

MESH = pl.DeviceIdType.MESH
F32, BF16 = jnp.float32, jnp.bfloat16
NT = (((1,), (1,)), ((), ()))
X, Y, Z = 4, 4, 8
NB = X * Y * Z
T = 1024
D = 256
G = 128
H = T // 2
RADIUS = 1.25 * math.sqrt(2.0 * D) / math.sqrt(2.0)
M1, OWN, P1, M2, P2 = range(5)
TILE_OF = (1, 2, 3, 0, 4)
UP, DOWN = 5, 6
COPIES = (
    (OWN, 1, 1, M1),
    (OWN, 0, -1, P1),
    (OWN, 0, 1, M1),
    (OWN, 1, -1, P1),
    (M1, 1, 1, M2),
    (P1, 0, -1, P2),
    (P2, 0, X, M2),
    (M2, 1, -X, P2),
    (OWN, 0, "y+", UP),
    (OWN, 1, "y-", DOWN),
    (UP, 0, "y- +1", M1),
    (DOWN, 1, "y+ -1", P1),
)
SEMS = (0, 1, 2, 3, 4, 5, 6, 7, 8, 9, 2, 3)


def kernel(
    f_hbm, t_hbm, n_ref, pat_ref, sol_hbm, res_hbm, img_hbm,
    f32, t32, f_low, fn, f_relay, na, ktile, diag, nb, e_relay, cur, w1s, w2s, r1s, obuf, coef, xb, yb, zb,
    in_sem, out_sem, f_send, f_recv, sib_send, sib_recv, e_send, e_recv, ar_send, ar_recv,
):
    r, c = lax.axis_index("rows"), lax.axis_index("out")
    x, y, z = lax.rem(r, X), lax.rem(r // X, Y), r // (X * Y)

    def at(step):
        return (lax.rem(r + step + NB, NB), c)

    def along(axis, d):
        if axis == 0:
            return ((z * Y + y) * X + lax.rem(x + d, X), c)
        if axis == 1:
            return ((z * Y + lax.rem(y + d, Y)) * X + x, c)
        return ((lax.rem(z + d, Z) * Y + y) * X + x, c)

    def target(to):
        if isinstance(to, int):
            return at(to)
        if len(to) == 2:
            return along(1, 1 if to == "y+" else Y - 1)
        up = to == "y- +1"
        row, _ = along(1, Y - 1 if up else 1)
        return (lax.rem(row + (1 if up else NB - 1), NB), c)

    sibling = (r, 1 - c)
    load_f = pltpu.make_async_copy(f_hbm, f32, in_sem.at[0])
    load_t = pltpu.make_async_copy(t_hbm, t32, in_sem.at[1])
    load_f.start()
    load_t.start()

    barrier = pltpu.get_barrier_semaphore()
    peers = [at(1), at(-1), at(X), at(-X), at(X * Y - X + 1), at(X - X * Y - 1), sibling]
    for axis, size in enumerate((X, Y, Z)):
        peers += [along(axis, d) for d in range(1, size)]
    for peer in peers:
        pl.semaphore_signal(barrier, inc=1, device_id=peer, device_id_type=MESH)

    def feature_rows(half):
        return pl.ds(pl.multiple_of(c * H + half * (H // 2), H // 2), H // 2)

    def f_copy(i):
        src, half, to, dst = COPIES[i]
        rows = feature_rows(half)

        def ref(slot):
            return f_relay.at[slot - UP] if slot >= UP else fn.at[slot, rows]

        return pltpu.make_async_remote_copy(
            src_ref=ref(src), dst_ref=ref(dst),
            send_sem=f_send.at[SEMS[i]], recv_sem=f_recv.at[SEMS[i]],
            device_id=target(to), device_id_type=MESH,
        )

    def s_copy(slot):
        rows = pl.ds(pl.multiple_of(c * H, H), H)
        return pltpu.make_async_remote_copy(
            src_ref=fn.at[slot, rows], dst_ref=fn.at[slot, rows],
            send_sem=sib_send.at[slot], recv_sem=sib_recv.at[slot],
            device_id=sibling, device_id_type=MESH,
        )

    def e_copy(s, i):
        src, half, to, dst = COPIES[i]
        rows = pl.ds(half * H, H)

        def ref(slot):
            return e_relay.at[s, slot - UP] if slot >= UP else nb.at[s, slot, rows]

        return pltpu.make_async_remote_copy(
            src_ref=ref(src), dst_ref=ref(dst),
            send_sem=e_send.at[s, SEMS[i]], recv_sem=e_recv.at[s, SEMS[i]],
            device_id=target(to), device_id_type=MESH,
        )

    def send(copy):
        copy(0).start()
        copy(1).start()

        @pl.when(x == X - 1)
        def _():
            copy(8).start()

        @pl.when(x < X - 1)
        def _():
            copy(2).start()

        @pl.when(x == 0)
        def _():
            copy(9).start()

        @pl.when(x > 0)
        def _():
            copy(3).start()

    def forward(copy):
        copy(0).wait_recv()
        copy(4).start()
        copy(1).wait_recv()
        copy(5).start()

        @pl.when(x == X - 1)
        def _():
            copy(8).wait_recv()
            copy(10).start()

        @pl.when(x == 0)
        def _():
            copy(9).wait_recv()
            copy(11).start()

    def swap(copy):
        copy(4).wait_recv()
        copy(7).start()
        copy(5).wait_recv()
        copy(6).start()

    def drain(copy):
        for i in range(8):
            copy(i).wait_send()

        @pl.when(x == X - 1)
        def _():
            copy(8).wait_send()

        @pl.when(x == 0)
        def _():
            copy(9).wait_send()

    def exchange(s):
        return functools.partial(e_copy, s)

    def ar_buf(axis, k):
        return ((xb, x), (yb, y), (zb, z))[axis]

    def ar_copies(k, axis):
        buf, own = ar_buf(axis, k)
        first = (0, X - 1, X + Y - 2)[axis]
        return [
            pltpu.make_async_remote_copy(
                src_ref=buf.at[k, own], dst_ref=buf.at[k, own],
                send_sem=ar_send.at[k, first + d - 1], recv_sem=ar_recv.at[k, first + d - 1],
                device_id=along(axis, d), device_id_type=MESH,
            )
            for d in range(1, (X, Y, Z)[axis])
        ]

    def ar_start(k, axis, value):
        buf, own = ar_buf(axis, k)
        buf[k, own] = value
        for copy in ar_copies(k, axis):
            copy.start()

    def ar_finish(k, axis):
        for copy in ar_copies(k, axis):
            copy.wait_recv()
        buf, _ = ar_buf(axis, k)
        total = buf[k, 0]
        for i in range(1, (X, Y, Z)[axis]):
            total = total + buf[k, i]
        return total

    load_f.wait()
    fn[OWN] = f32[...].astype(BF16)
    pl.semaphore_wait(barrier, len(peers))
    send(f_copy)
    f_low[...] = (f32[...] - fn[OWN].astype(F32)).astype(BF16)
    load_t.wait()
    for g in range(2):
        nb[g, OWN] = t32[:, g * G:(g + 1) * G].astype(BF16)
        cur[g] = t32[:, g * G:(g + 1) * G]

    def squares(block, parts):
        wide = block.astype(F32)
        rest = wide * wide
        found = []
        for _ in range(parts):
            found.append(rest.astype(BF16))
            rest = rest - found[-1].astype(F32)
        return found

    def dot_nt(a, b):
        return lax.dot_general(a, b, NT, preferred_element_type=F32)

    halves_col = jnp.full((D, G), 0.5, BF16)
    halves_row = jnp.full((16, D), 0.5, BF16)
    own_squares = squares(f32[...], 3)
    na[...] = sum(jnp.dot(part, halves_col, preferred_element_type=F32) for part in own_squares)
    diag[...] = jnp.zeros_like(diag)

    def build(slot):
        own = slot == OWN
        other = fn[slot]
        parts = own_squares if own else squares(other, 2)
        norms = sum(dot_nt(halves_row, part) for part in parts)
        kept = pat_ref[0, TILE_OF[slot]].astype(F32)
        base = kept * (1.0 / (RADIUS**4 * T))
        slope = kept * (4.0 / (RADIUS**5 * T))
        split = jnp.concatenate([fn[OWN], f_low[...]], axis=1)
        cross = dot_nt(split, jnp.concatenate([other, other], axis=1))
        if own:
            cross = cross + dot_nt(split, jnp.concatenate([f_low[...], f_low[...]], axis=1))
        norm = na[...]
        summed = diag[...]
        for lane in range(T // G):
            cols = slice(lane * G, (lane + 1) * G)
            half_sq = jnp.maximum(norm + norms[0:1, cols] - cross[:, cols], 1e-30)
            dist = half_sq * lax.rsqrt(half_sq)
            fall = jnp.maximum(RADIUS - dist, 0.0)
            fall = fall * fall
            value = (fall * fall) * (dist * slope + base)
            start = slot * T + lane * G
            ktile[:, start:start + G] = value.astype(BF16)
            summed = summed + value
        diag[...] = summed

    build(OWN)
    forward(f_copy)
    send(exchange(0))
    f_copy(2).wait_recv()
    s_copy(M1).start()
    f_copy(3).wait_recv()
    s_copy(P1).start()
    s_copy(M1).wait_recv()
    build(M1)
    swap(f_copy)
    s_copy(P1).wait_recv()
    build(P1)
    forward(exchange(0))
    send(exchange(1))
    f_copy(6).wait_recv()
    s_copy(M2).start()
    f_copy(7).wait_recv()
    s_copy(P2).start()
    s_copy(M2).wait_recv()
    build(M2)
    swap(exchange(0))
    s_copy(P2).wait_recv()
    build(P2)
    nugget = jnp.broadcast_to(n_ref[0:1, :], (G, T)).T
    diag[...] = nugget + jnp.sum(diag[...], axis=1, keepdims=True)

    def out_copy(g, i):
        cols = pl.ds(pl.multiple_of(g * G, G), G)
        out = (sol_hbm, res_hbm, img_hbm)[i]
        return pltpu.make_async_copy(obuf.at[g, i], out.at[:, cols], out_sem.at[g, i])

    def step(s, _):
        g, e = lax.rem(s, 2), s // 2
        cols = pl.ds(pl.multiple_of(g * G, G), G)

        def product(first, last):
            return jnp.dot(
                ktile[:, first * T:(last + 1) * T],
                nb[s, first:last + 1].reshape((last + 1 - first) * T, G),
                preferred_element_type=F32,
            )

        e_copy(s, 2).wait_recv()
        e_copy(s, 3).wait_recv()
        w2s[g] = diag[...] * cur[g] + product(M1, P1)

        @pl.when(s >= 1)
        def _():
            swap(exchange(s))

        @pl.when(s <= 4)
        def _():
            forward(exchange(s + 1))

        @pl.when((s >= 1) & (s <= 4))
        def _():
            ar_start(s - 1, 1, ar_finish(s - 1, 0))

        @pl.when(e == 2)
        def _():
            total = ar_finish(s - 2, 2)
            norm, cross = total[0:1, :], total[1:2, :]
            step0 = coef[g, 1:2, :]
            momentum = norm / coef[g, 0:1, :]
            step1 = norm / (cross - momentum * norm / step0)
            coef[g, 2:3, :] = momentum
            coef[g, 3:4, :] = step1
            start = t32[:, cols]
            res = r1s[g]
            obuf[g, 0] = step0 * start + step1 * (res + momentum * start)
            obuf[g, 1] = res - step1 * (cur[g] + momentum * w1s[g])
            out_copy(g, 0).start()
            out_copy(g, 1).start()

        e_copy(s, 6).wait_recv()
        e_copy(s, 7).wait_recv()
        w2s[g] = w2s[g] + product(M2, P2)

        def reduce_start(norm, cross):
            ar_start(s, 0, jnp.concatenate(
                [jnp.sum(norm, axis=0, keepdims=True), jnp.sum(cross, axis=0, keepdims=True),
                 jnp.zeros((6, G), F32)], axis=0))

        @pl.when(e == 0)
        def _():
            w = w2s[g]
            nb[s + 2, OWN] = w.astype(BF16)
            send(exchange(s + 2))
            start = t32[:, cols]
            cur[g] = w
            w1s[g] = w
            reduce_start(start * start, w * start)

        @pl.when(e == 1)
        def _():
            total = ar_finish(s - 2, 2)
            norm, cross = total[0:1, :], total[1:2, :]
            step0 = norm / cross
            coef[g, 0:1, :] = norm
            coef[g, 1:2, :] = step0
            image = cur[g] - step0 * w2s[g]
            nb[s + 2, OWN] = image.astype(BF16)
            send(exchange(s + 2))
            cur[g] = image
            res = t32[:, cols] - step0 * w1s[g]
            r1s[g] = res
            obuf[g, 2] = w2s[g]
            reduce_start(res * res, image * res)

        @pl.when(e == 2)
        def _():
            momentum, step1 = coef[g, 2:3, :], coef[g, 3:4, :]
            obuf[g, 2] = cur[g] - step1 * (w2s[g] + momentum * obuf[g, 2])
            out_copy(g, 2).start()

        @pl.when((s >= 1) & (s <= 4))
        def _():
            ar_start(s - 1, 2, ar_finish(s - 1, 1))

        return 0

    lax.fori_loop(0, 6, step, 0)

    drain(f_copy)
    for slot in (M1, P1, M2, P2):
        s_copy(slot).wait_send()

    def finish(s, _):
        drain(exchange(s))

        @pl.when(s < 4)
        def _():
            for axis in range(3):
                for copy in ar_copies(s, axis):
                    copy.wait_send()

        @pl.when(s < 2)
        def _():
            for i in range(3):
                out_copy(s, i).wait()

        return 0

    lax.fori_loop(0, 6, finish, 0)


def body(features, targets, nugget, pattern):
    out = jax.ShapeDtypeStruct((T, 2 * G), F32)
    dma = pltpu.SemaphoreType.DMA
    return pl.pallas_call(
        kernel,
        out_shape=(out, out, out),
        in_specs=[
            pl.BlockSpec(memory_space=pl.ANY),
            pl.BlockSpec(memory_space=pl.ANY),
            pl.BlockSpec(memory_space=pltpu.VMEM),
            pl.BlockSpec(memory_space=pltpu.SMEM),
        ],
        out_specs=(pl.BlockSpec(memory_space=pl.ANY),) * 3,
        scratch_shapes=[
            pltpu.VMEM((T, D), F32),
            pltpu.VMEM((T, 2 * G), F32),
            pltpu.VMEM((T, D), BF16),
            pltpu.VMEM((5, T, D), BF16),
            pltpu.VMEM((2, H // 2, D), BF16),
            pltpu.VMEM((T, G), F32),
            pltpu.VMEM((T, 5 * T), BF16),
            pltpu.VMEM((T, G), F32),
            pltpu.VMEM((6, 5, T, G), BF16),
            pltpu.VMEM((6, 2, H, G), BF16),
            pltpu.VMEM((2, T, G), F32),
            pltpu.VMEM((2, T, G), F32),
            pltpu.VMEM((2, T, G), F32),
            pltpu.VMEM((2, T, G), F32),
            pltpu.VMEM((2, 3, T, G), F32),
            pltpu.VMEM((2, 8, G), F32),
            pltpu.VMEM((4, X, 8, G), F32),
            pltpu.VMEM((4, Y, 8, G), F32),
            pltpu.VMEM((4, Z, 8, G), F32),
            dma((2,)),
            dma((2, 3)),
            dma((10,)),
            dma((10,)),
            dma((5,)),
            dma((5,)),
            dma((6, 10)),
            dma((6, 10)),
            dma((4, X + Y + Z - 3)),
            dma((4, X + Y + Z - 3)),
        ],
        compiler_params=pltpu.CompilerParams(
            collective_id=0, has_side_effects=True, vmem_limit_bytes=56 * 2**20
        ),
        name="cascaded_cg",
    )(features, targets, nugget.reshape(1, T), pattern)


def solution(mesh):
    return jax.shard_map(
        body,
        mesh=mesh,
        in_specs=(P("rows", None), P("rows", "out"), P("rows"), P("rows", None)),
        out_specs=(P("rows", "out"), P("rows", "out"), P("rows", "out")),
        check_vma=False,
    )
```

```python
import functools
import math

import jax
import jax.numpy as jnp
from jax import lax
from jax.experimental import pallas as pl
from jax.experimental.pallas import tpu as pltpu
from jax.sharding import PartitionSpec as P

MESH = pl.DeviceIdType.MESH
F32, BF16 = jnp.float32, jnp.bfloat16
NT = (((1,), (1,)), ((), ()))
X, Y, Z = 4, 4, 8
NB = X * Y * Z
T = 1024
D = 256
G = 128
H = T // 2
RADIUS = 1.25 * math.sqrt(2.0 * D) / math.sqrt(2.0)
M1, OWN, P1, M2, P2 = range(5)
TILE_OF = (1, 2, 3, 0, 4)
UP, DOWN = 5, 6
PLACE = {
    (M1, 1): 0, (OWN, 0): 1, (OWN, 1): 2, (P1, 0): 3,
    (M1, 0): 4, (M2, 1): 5, (P2, 0): 6, (P1, 1): 7,
    (M2, 0): 8, (P2, 1): 9,
}
COPIES = (
    (OWN, 1, 1, M1),
    (OWN, 0, -1, P1),
    (OWN, 0, 1, M1),
    (OWN, 1, -1, P1),
    (M1, 1, 1, M2),
    (P1, 0, -1, P2),
    (P2, 0, X, M2),
    (M2, 1, -X, P2),
    (OWN, 0, "y+", UP),
    (OWN, 1, "y-", DOWN),
    (UP, 0, "y- +1", M1),
    (DOWN, 1, "y+ -1", P1),
)
SEMS = (0, 1, 2, 3, 4, 5, 6, 7, 8, 9, 2, 3)


def kernel(
    f_hbm, t_hbm, n_ref, pat_ref, sol_hbm, res_hbm, img_hbm,
    f32, t32, f_low, fn, na, ktile, diag, nb, e_relay, cur, w1s, w2s, r1s, obuf, coef, xb, yb, zb,
    in_sem, out_sem, f_send, f_recv, sib_send, sib_recv, e_send, e_recv, ar_send, ar_recv,
):
    r, c = lax.axis_index("rows"), lax.axis_index("out")
    x, y, z = lax.rem(r, X), lax.rem(r // X, Y), r // (X * Y)

    def at(step):
        return (lax.rem(r + step + NB, NB), c)

    def along(axis, d):
        if axis == 0:
            return ((z * Y + y) * X + lax.rem(x + d, X), c)
        if axis == 1:
            return ((z * Y + lax.rem(y + d, Y)) * X + x, c)
        return ((lax.rem(z + d, Z) * Y + y) * X + x, c)

    def target(to):
        if isinstance(to, int):
            return at(to)
        if len(to) == 2:
            return along(1, 1 if to == "y+" else Y - 1)
        up = to == "y- +1"
        row, _ = along(1, Y - 1 if up else 1)
        return (lax.rem(row + (1 if up else NB - 1), NB), c)

    sibling = (r, 1 - c)
    load_f = pltpu.make_async_copy(f_hbm, f32, in_sem.at[0])
    load_t = pltpu.make_async_copy(t_hbm, t32, in_sem.at[1])
    load_f.start()
    load_t.start()

    barrier = pltpu.get_barrier_semaphore()
    peers = [at(1), at(-1), at(X), at(-X), at(X * Y - X + 1), at(X - X * Y - 1), sibling]
    for axis, size in enumerate((X, Y, Z)):
        peers += [along(axis, d) for d in range(1, size)]
    for peer in peers:
        pl.semaphore_signal(barrier, inc=1, device_id=peer, device_id_type=MESH)

    def feature_rows(half):
        return pl.ds(pl.multiple_of(c * H + half * (H // 2), H // 2), H // 2)

    def f_copy(i):
        src, half, to, dst = COPIES[i]
        rows = feature_rows(half)

        return pltpu.make_async_remote_copy(
            src_ref=fn.at[src, rows], dst_ref=fn.at[dst, rows],
            send_sem=f_send.at[i], recv_sem=f_recv.at[i],
            device_id=target(to), device_id_type=MESH,
        )

    def s_copy(slot):
        rows = pl.ds(pl.multiple_of(c * H, H), H)
        return pltpu.make_async_remote_copy(
            src_ref=fn.at[slot, rows], dst_ref=fn.at[slot, rows],
            send_sem=sib_send.at[slot], recv_sem=sib_recv.at[slot],
            device_id=sibling, device_id_type=MESH,
        )

    def e_copy(s, i):
        src, half, to, dst = COPIES[i]

        def ref(slot):
            return e_relay.at[s, slot - UP] if slot >= UP else nb.at[s, PLACE[slot, half]]

        return pltpu.make_async_remote_copy(
            src_ref=ref(src), dst_ref=ref(dst),
            send_sem=e_send.at[s, SEMS[i]], recv_sem=e_recv.at[s, SEMS[i]],
            device_id=target(to), device_id_type=MESH,
        )

    def put(s, field):
        for half in range(2):
            nb[s, PLACE[OWN, half]] = field[half * H:(half + 1) * H].astype(BF16)

    def send(copy):
        copy(0).start()
        copy(1).start()

        @pl.when(x == X - 1)
        def _():
            copy(8).start()

        @pl.when(x < X - 1)
        def _():
            copy(2).start()

        @pl.when(x == 0)
        def _():
            copy(9).start()

        @pl.when(x > 0)
        def _():
            copy(3).start()

    def forward(copy, relayed=True):
        copy(0).wait_recv()
        copy(4).start()
        copy(1).wait_recv()
        copy(5).start()
        if not relayed:
            return

        @pl.when(x == X - 1)
        def _():
            copy(8).wait_recv()
            copy(10).start()

        @pl.when(x == 0)
        def _():
            copy(9).wait_recv()
            copy(11).start()

    def swap(copy):
        copy(4).wait_recv()
        copy(7).start()
        copy(5).wait_recv()
        copy(6).start()

    def drain(copy):
        for i in range(8):
            copy(i).wait_send()

        @pl.when(x == X - 1)
        def _():
            copy(8).wait_send()

        @pl.when(x == 0)
        def _():
            copy(9).wait_send()

    def exchange(s):
        return functools.partial(e_copy, s)

    def ar_buf(axis, k):
        return ((xb, x), (yb, y), (zb, z))[axis]

    def ar_copies(k, axis):
        buf, own = ar_buf(axis, k)
        first = (0, X - 1, X + Y - 2)[axis]
        return [
            pltpu.make_async_remote_copy(
                src_ref=buf.at[k, own], dst_ref=buf.at[k, own],
                send_sem=ar_send.at[k, first + d - 1], recv_sem=ar_recv.at[k, first + d - 1],
                device_id=along(axis, d), device_id_type=MESH,
            )
            for d in range(1, (X, Y, Z)[axis])
        ]

    def ar_start(k, axis, value):
        buf, own = ar_buf(axis, k)
        buf[k, own] = value
        for copy in ar_copies(k, axis):
            copy.start()

    def ar_finish(k, axis):
        for copy in ar_copies(k, axis):
            copy.wait_recv()
        buf, _ = ar_buf(axis, k)
        total = buf[k, 0]
        for i in range(1, (X, Y, Z)[axis]):
            total = total + buf[k, i]
        return total

    load_f.wait()
    fn[OWN] = f32[...].astype(BF16)
    pl.semaphore_wait(barrier, len(peers))
    for i in range(4):
        f_copy(i).start()
    f_low[...] = (f32[...] - fn[OWN].astype(F32)).astype(BF16)
    load_t.wait()
    for g in range(2):
        put(g, t32[:, g * G:(g + 1) * G])
        cur[g] = t32[:, g * G:(g + 1) * G]

    def squares(block, parts):
        wide = block.astype(F32)
        rest = wide * wide
        found = []
        for _ in range(parts):
            found.append(rest.astype(BF16))
            rest = rest - found[-1].astype(F32)
        return found

    def dot_nt(a, b):
        return lax.dot_general(a, b, NT, preferred_element_type=F32)

    halves_col = jnp.full((D, G), 0.5, BF16)
    halves_row = jnp.full((16, D), 0.5, BF16)
    own_squares = squares(f32[...], 3)
    na[...] = sum(jnp.dot(part, halves_col, preferred_element_type=F32) for part in own_squares)
    diag[...] = jnp.zeros_like(diag)

    def build(slot):
        own = slot == OWN
        other = fn[slot]
        parts = own_squares if own else squares(other, 2)
        norms = sum(dot_nt(halves_row, part) for part in parts)
        kept = pat_ref[0, TILE_OF[slot]].astype(F32)
        base = kept * (1.0 / (RADIUS**4 * T))
        slope = kept * (4.0 / (RADIUS**5 * T))
        split = jnp.concatenate([fn[OWN], f_low[...]], axis=1)
        cross = dot_nt(split, jnp.concatenate([other, other], axis=1))
        if own:
            cross = cross + dot_nt(split, jnp.concatenate([f_low[...], f_low[...]], axis=1))
        norm = na[...]
        summed = diag[...]
        for lane in range(T // G):
            cols = slice(lane * G, (lane + 1) * G)
            half_sq = jnp.maximum(norm + norms[0:1, cols] - cross[:, cols], 1e-30)
            dist = half_sq * lax.rsqrt(half_sq)
            fall = jnp.maximum(RADIUS - dist, 0.0)
            fall = fall * fall
            value = (fall * fall) * (dist * slope + base)
            start = PLACE[slot, lane * G // H] * H + lane * G % H
            ktile[:, start:start + G] = value.astype(BF16)
            summed = summed + value
        diag[...] = summed

    build(OWN)
    forward(f_copy, relayed=False)
    send(exchange(0))
    f_copy(2).wait_recv()
    s_copy(M1).start()
    f_copy(3).wait_recv()
    s_copy(P1).start()
    s_copy(M1).wait_recv()
    build(M1)
    swap(f_copy)
    s_copy(P1).wait_recv()
    build(P1)
    forward(exchange(0))
    send(exchange(1))
    f_copy(6).wait_recv()
    s_copy(M2).start()
    f_copy(7).wait_recv()
    s_copy(P2).start()
    s_copy(M2).wait_recv()
    build(M2)
    swap(exchange(0))
    s_copy(P2).wait_recv()
    build(P2)
    nugget = jnp.broadcast_to(n_ref[0:1, :], (G, T)).T
    diag[...] = nugget + jnp.sum(diag[...], axis=1, keepdims=True)

    def out_copy(g, i):
        cols = pl.ds(pl.multiple_of(g * G, G), G)
        out = (sol_hbm, res_hbm, img_hbm)[i]
        return pltpu.make_async_copy(obuf.at[g, i], out.at[:, cols], out_sem.at[g, i])

    def step(s, _):
        g, e = lax.rem(s, 2), s // 2
        cols = pl.ds(pl.multiple_of(g * G, G), G)

        def product(first, last):
            return jnp.dot(
                ktile[:, first * H:last * H],
                nb[s, first:last].reshape((last - first) * H, G),
                preferred_element_type=F32,
            )

        w2s[g] = diag[...] * cur[g] + product(0, 4)

        @pl.when(s >= 1)
        def _():
            swap(exchange(s))

        @pl.when(s <= 4)
        def _():
            forward(exchange(s + 1))

        e_copy(s, 2).wait_recv()
        e_copy(s, 3).wait_recv()
        w2s[g] = w2s[g] + product(4, 8)

        @pl.when((s >= 1) & (s <= 4))
        def _():
            ar_start(s - 1, 1, ar_finish(s - 1, 0))

        @pl.when(e == 2)
        def _():
            total = ar_finish(s - 2, 2)
            norm, cross = total[0:1, :], total[1:2, :]
            step0 = coef[g, 1:2, :]
            momentum = norm / coef[g, 0:1, :]
            step1 = norm / (cross - momentum * norm / step0)
            coef[g, 2:3, :] = momentum
            coef[g, 3:4, :] = step1
            start = t32[:, cols]
            res = r1s[g]
            obuf[g, 0] = step0 * start + step1 * (res + momentum * start)
            obuf[g, 1] = res - step1 * (cur[g] + momentum * w1s[g])
            out_copy(g, 0).start()
            out_copy(g, 1).start()

        e_copy(s, 6).wait_recv()
        e_copy(s, 7).wait_recv()
        w2s[g] = w2s[g] + product(8, 10)

        def reduce_start(norm, cross):
            ar_start(s, 0, jnp.concatenate(
                [jnp.sum(norm, axis=0, keepdims=True), jnp.sum(cross, axis=0, keepdims=True),
                 jnp.zeros((6, G), F32)], axis=0))

        @pl.when(e == 0)
        def _():
            w = w2s[g]
            put(s + 2, w)
            send(exchange(s + 2))
            start = t32[:, cols]
            cur[g] = w
            w1s[g] = w
            reduce_start(start * start, w * start)

        @pl.when(e == 1)
        def _():
            total = ar_finish(s - 2, 2)
            norm, cross = total[0:1, :], total[1:2, :]
            step0 = norm / cross
            coef[g, 0:1, :] = norm
            coef[g, 1:2, :] = step0
            image = cur[g] - step0 * w2s[g]
            put(s + 2, image)
            send(exchange(s + 2))
            cur[g] = image
            res = t32[:, cols] - step0 * w1s[g]
            r1s[g] = res
            obuf[g, 2] = w2s[g]
            reduce_start(res * res, image * res)

        @pl.when(e == 2)
        def _():
            momentum, step1 = coef[g, 2:3, :], coef[g, 3:4, :]
            obuf[g, 2] = cur[g] - step1 * (w2s[g] + momentum * obuf[g, 2])
            out_copy(g, 2).start()

        @pl.when((s >= 1) & (s <= 4))
        def _():
            ar_start(s - 1, 2, ar_finish(s - 1, 1))

        return 0

    lax.fori_loop(0, 6, step, 0)

    for i in range(8):
        f_copy(i).wait_send()
    for slot in (M1, P1, M2, P2):
        s_copy(slot).wait_send()

    def finish(s, _):
        drain(exchange(s))

        @pl.when(s < 4)
        def _():
            for axis in range(3):
                for copy in ar_copies(s, axis):
                    copy.wait_send()

        @pl.when(s < 2)
        def _():
            for i in range(3):
                out_copy(s, i).wait()

        return 0

    lax.fori_loop(0, 6, finish, 0)


def body(features, targets, nugget, pattern):
    out = jax.ShapeDtypeStruct((T, 2 * G), F32)
    inputs = (features, targets, nugget.reshape(1, T), pattern)
    dma = pltpu.SemaphoreType.DMA
    return pl.pallas_call(
        kernel,
        out_shape=(out, out, out),
        in_specs=[
            pl.BlockSpec(memory_space=pl.ANY),
            pl.BlockSpec(memory_space=pl.ANY),
            pl.BlockSpec(memory_space=pltpu.VMEM),
            pl.BlockSpec(memory_space=pltpu.SMEM),
        ],
        out_specs=(pl.BlockSpec(memory_space=pl.ANY),) * 3,
        scratch_shapes=[
            pltpu.VMEM((T, D), F32),
            pltpu.VMEM((T, 2 * G), F32),
            pltpu.VMEM((T, D), BF16),
            pltpu.VMEM((5, T, D), BF16),
            pltpu.VMEM((T, G), F32),
            pltpu.VMEM((T, 5 * T), BF16),
            pltpu.VMEM((T, G), F32),
            pltpu.VMEM((6, 10, H, G), BF16),
            pltpu.VMEM((6, 2, H, G), BF16),
            pltpu.VMEM((2, T, G), F32),
            pltpu.VMEM((2, T, G), F32),
            pltpu.VMEM((2, T, G), F32),
            pltpu.VMEM((2, T, G), F32),
            pltpu.VMEM((2, 3, T, G), F32),
            pltpu.VMEM((2, 8, G), F32),
            pltpu.VMEM((4, X, 8, G), F32),
            pltpu.VMEM((4, Y, 8, G), F32),
            pltpu.VMEM((4, Z, 8, G), F32),
            dma((2,)),
            dma((2, 3)),
            dma((8,)),
            dma((8,)),
            dma((5,)),
            dma((5,)),
            dma((6, 10)),
            dma((6, 10)),
            dma((4, X + Y + Z - 3)),
            dma((4, X + Y + Z - 3)),
        ],
        compiler_params=pltpu.CompilerParams(
            collective_id=0, has_side_effects=True, vmem_limit_bytes=46 * 2**20
        ),
        name="cascaded_cg",
    )(*(pltpu.with_memory_space_constraint(array, pltpu.HBM) for array in inputs))


def solution(mesh):
    return jax.shard_map(
        body,
        mesh=mesh,
        in_specs=(P("rows", None), P("rows", "out"), P("rows"), P("rows", None)),
        out_specs=(P("rows", "out"), P("rows", "out"), P("rows", "out")),
        check_vma=False,
    )
```

```python
import functools
import math

import jax
import jax.numpy as jnp
from jax import lax
from jax.experimental import pallas as pl
from jax.experimental.pallas import tpu as pltpu
from jax.sharding import PartitionSpec as P

MESH = pl.DeviceIdType.MESH
F32, BF16 = jnp.float32, jnp.bfloat16
NT = (((1,), (1,)), ((), ()))
X, Y, Z = 4, 4, 8
NB = X * Y * Z
T = 1024
D = 256
G = 128
H = T // 2
RADIUS = 1.25 * math.sqrt(2.0 * D) / math.sqrt(2.0)
M1, OWN, P1, M2, P2 = range(5)
TILE_OF = (1, 2, 3, 0, 4)
UP, DOWN = 5, 6
PLACE = {
    (M1, 1): 0, (OWN, 0): 1, (OWN, 1): 2, (P1, 0): 3,
    (M1, 0): 4, (M2, 1): 5, (P2, 0): 6, (P1, 1): 7,
    (M2, 0): 8, (P2, 1): 9,
}
COPIES = (
    (OWN, 1, 1, M1),
    (OWN, 0, -1, P1),
    (OWN, 0, 1, M1),
    (OWN, 1, -1, P1),
    (M1, 1, 1, M2),
    (P1, 0, -1, P2),
    (P2, 0, X, M2),
    (M2, 1, -X, P2),
    (OWN, 0, "y+", UP),
    (OWN, 1, "y-", DOWN),
    (UP, 0, "y- +1", M1),
    (DOWN, 1, "y+ -1", P1),
)
SEMS = (0, 1, 2, 3, 4, 5, 6, 7, 8, 9, 2, 3)


def kernel(
    f_hbm, t_hbm, n_ref, pat_ref, sol_ref, res_ref, img_ref,
    f32, t32, f_low, fn, na, ktile, diag, nb, e_relay, cur, w1s, w2s, r1s, steps, coef, xb, yb, zb,
    in_sem, f_send, f_recv, sib_send, sib_recv, e_send, e_recv, ar_send, ar_recv,
):
    r, c = lax.axis_index("rows"), lax.axis_index("out")
    x, y, z = lax.rem(r, X), lax.rem(r // X, Y), r // (X * Y)

    def at(step):
        return (lax.rem(r + step + NB, NB), c)

    def along(axis, d):
        if axis == 0:
            return ((z * Y + y) * X + lax.rem(x + d, X), c)
        if axis == 1:
            return ((z * Y + lax.rem(y + d, Y)) * X + x, c)
        return ((lax.rem(z + d, Z) * Y + y) * X + x, c)

    def target(to):
        if isinstance(to, int):
            return at(to)
        if len(to) == 2:
            return along(1, 1 if to == "y+" else Y - 1)
        up = to == "y- +1"
        row, _ = along(1, Y - 1 if up else 1)
        return (lax.rem(row + (1 if up else NB - 1), NB), c)

    sibling = (r, 1 - c)
    load_f = pltpu.make_async_copy(f_hbm, f32, in_sem.at[0])
    load_t = pltpu.make_async_copy(t_hbm, t32, in_sem.at[1])
    load_f.start()
    load_t.start()

    barrier = pltpu.get_barrier_semaphore()
    peers = [at(1), at(-1), at(X), at(-X), at(X * Y - X + 1), at(X - X * Y - 1), sibling]
    for axis, size in enumerate((X, Y, Z)):
        peers += [along(axis, d) for d in range(1, size)]
    for peer in peers:
        pl.semaphore_signal(barrier, inc=1, device_id=peer, device_id_type=MESH)

    def feature_rows(half):
        return pl.ds(pl.multiple_of(c * H + half * (H // 2), H // 2), H // 2)

    def f_copy(i):
        src, half, to, dst = COPIES[i]
        rows = feature_rows(half)

        return pltpu.make_async_remote_copy(
            src_ref=fn.at[src, rows], dst_ref=fn.at[dst, rows],
            send_sem=f_send.at[i], recv_sem=f_recv.at[i],
            device_id=target(to), device_id_type=MESH,
        )

    def s_copy(slot):
        rows = pl.ds(pl.multiple_of(c * H, H), H)
        return pltpu.make_async_remote_copy(
            src_ref=fn.at[slot, rows], dst_ref=fn.at[slot, rows],
            send_sem=sib_send.at[slot], recv_sem=sib_recv.at[slot],
            device_id=sibling, device_id_type=MESH,
        )

    def e_copy(s, i):
        src, half, to, dst = COPIES[i]

        def ref(slot):
            return e_relay.at[s, slot - UP] if slot >= UP else nb.at[s, PLACE[slot, half]]

        return pltpu.make_async_remote_copy(
            src_ref=ref(src), dst_ref=ref(dst),
            send_sem=e_send.at[s, SEMS[i]], recv_sem=e_recv.at[s, SEMS[i]],
            device_id=target(to), device_id_type=MESH,
        )

    def put(s, field):
        for half in range(2):
            nb[s, PLACE[OWN, half]] = field[half * H:(half + 1) * H].astype(BF16)

    def send(copy):
        copy(0).start()
        copy(1).start()

        @pl.when(x == X - 1)
        def _():
            copy(8).start()

        @pl.when(x < X - 1)
        def _():
            copy(2).start()

        @pl.when(x == 0)
        def _():
            copy(9).start()

        @pl.when(x > 0)
        def _():
            copy(3).start()

    def forward(copy, relayed=True):
        copy(0).wait_recv()
        copy(4).start()
        copy(1).wait_recv()
        copy(5).start()
        if not relayed:
            return

        @pl.when(x == X - 1)
        def _():
            copy(8).wait_recv()
            copy(10).start()

        @pl.when(x == 0)
        def _():
            copy(9).wait_recv()
            copy(11).start()

    def swap(copy):
        copy(4).wait_recv()
        copy(7).start()
        copy(5).wait_recv()
        copy(6).start()

    def drain(copy):
        for i in range(8):
            copy(i).wait_send()

        @pl.when(x == X - 1)
        def _():
            copy(8).wait_send()

        @pl.when(x == 0)
        def _():
            copy(9).wait_send()

    def exchange(s):
        return functools.partial(e_copy, s)

    def ar_buf(axis, k):
        return ((xb, x), (yb, y), (zb, z))[axis]

    def ar_copies(k, axis):
        buf, own = ar_buf(axis, k)
        first = (0, X - 1, X + Y - 2)[axis]
        return [
            pltpu.make_async_remote_copy(
                src_ref=buf.at[k, own], dst_ref=buf.at[k, own],
                send_sem=ar_send.at[k, first + d - 1], recv_sem=ar_recv.at[k, first + d - 1],
                device_id=along(axis, d), device_id_type=MESH,
            )
            for d in range(1, (X, Y, Z)[axis])
        ]

    def ar_start(k, axis, value):
        buf, own = ar_buf(axis, k)
        buf[k, own] = value
        for copy in ar_copies(k, axis):
            copy.start()

    def ar_finish(k, axis):
        for copy in ar_copies(k, axis):
            copy.wait_recv()
        buf, _ = ar_buf(axis, k)
        total = buf[k, 0]
        for i in range(1, (X, Y, Z)[axis]):
            total = total + buf[k, i]
        return total

    load_f.wait()
    fn[OWN] = f32[...].astype(BF16)
    pl.semaphore_wait(barrier, len(peers))
    for i in range(4):
        f_copy(i).start()
    f_low[...] = (f32[...] - fn[OWN].astype(F32)).astype(BF16)
    load_t.wait()
    for g in range(2):
        put(g, t32[:, g * G:(g + 1) * G])
        cur[g] = t32[:, g * G:(g + 1) * G]

    def squares(block, parts):
        wide = block.astype(F32)
        rest = wide * wide
        found = []
        for _ in range(parts):
            found.append(rest.astype(BF16))
            rest = rest - found[-1].astype(F32)
        return found

    def dot_nt(a, b):
        return lax.dot_general(a, b, NT, preferred_element_type=F32)

    halves_col = jnp.full((D, G), 0.5, BF16)
    halves_row = jnp.full((16, D), 0.5, BF16)
    own_squares = squares(f32[...], 3)
    na[...] = sum(jnp.dot(part, halves_col, preferred_element_type=F32) for part in own_squares)
    diag[...] = jnp.zeros_like(diag)

    def build(slot):
        own = slot == OWN
        other = fn[slot]
        parts = own_squares if own else squares(other, 2)
        norms = sum(dot_nt(halves_row, part) for part in parts)
        kept = pat_ref[0, TILE_OF[slot]].astype(F32)
        base = kept * (1.0 / (RADIUS**4 * T))
        slope = kept * (4.0 / (RADIUS**5 * T))
        split = jnp.concatenate([fn[OWN], f_low[...]], axis=1)
        cross = dot_nt(split, jnp.concatenate([other, other], axis=1))
        if own:
            cross = cross + dot_nt(split, jnp.concatenate([f_low[...], f_low[...]], axis=1))
        norm = na[...]
        summed = diag[...]
        for lane in range(T // G):
            cols = slice(lane * G, (lane + 1) * G)
            half_sq = jnp.maximum(norm + norms[0:1, cols] - cross[:, cols], 1e-30)
            dist = half_sq * lax.rsqrt(half_sq)
            fall = jnp.maximum(RADIUS - dist, 0.0)
            fall = fall * fall
            value = (fall * fall) * (dist * slope + base)
            start = PLACE[slot, lane * G // H] * H + lane * G % H
            ktile[:, start:start + G] = value.astype(BF16)
            summed = summed + value
        diag[...] = summed

    build(OWN)
    forward(f_copy, relayed=False)
    send(exchange(0))
    f_copy(2).wait_recv()
    s_copy(M1).start()
    f_copy(3).wait_recv()
    s_copy(P1).start()
    s_copy(M1).wait_recv()
    build(M1)
    swap(f_copy)
    s_copy(P1).wait_recv()
    build(P1)
    forward(exchange(0))
    send(exchange(1))
    f_copy(6).wait_recv()
    s_copy(M2).start()
    f_copy(7).wait_recv()
    s_copy(P2).start()
    s_copy(M2).wait_recv()
    build(M2)
    swap(exchange(0))
    s_copy(P2).wait_recv()
    build(P2)
    nugget = jnp.broadcast_to(n_ref[0:1, :], (G, T)).T
    diag[...] = nugget + jnp.sum(diag[...], axis=1, keepdims=True)

    def step(s, _):
        g, e = lax.rem(s, 2), s // 2
        cols = pl.ds(pl.multiple_of(g * G, G), G)

        def product(first, last):
            return jnp.dot(
                ktile[:, first * H:last * H],
                nb[s, first:last].reshape((last - first) * H, G),
                preferred_element_type=F32,
            )

        w2s[g] = diag[...] * cur[g] + product(0, 4)

        @pl.when(s >= 1)
        def _():
            swap(exchange(s))

        @pl.when(s <= 4)
        def _():
            forward(exchange(s + 1))

        e_copy(s, 2).wait_recv()
        e_copy(s, 3).wait_recv()
        w2s[g] = w2s[g] + product(4, 8)

        @pl.when((s >= 1) & (s <= 4))
        def _():
            ar_start(s - 1, 1, ar_finish(s - 1, 2))

        @pl.when(e == 2)
        def _():
            total = ar_finish(s - 2, 0)
            norm, cross = total[0:1, :], total[1:2, :]
            step0 = coef[g, 1:2, :]
            momentum = norm / coef[g, 0:1, :]
            step1 = norm / (cross - momentum * norm / step0)
            coef[g, 2:3, :] = momentum
            coef[g, 3:4, :] = step1
            start = t32[:, cols]
            res = r1s[g]
            sol_ref[:, cols] = step0 * start + step1 * (res + momentum * start)
            res_ref[:, cols] = res - step1 * (cur[g] + momentum * w1s[g])

        e_copy(s, 6).wait_recv()
        e_copy(s, 7).wait_recv()
        w2s[g] = w2s[g] + product(8, 10)

        def reduce_start(norm, cross):
            ar_start(s, 2, jnp.concatenate(
                [jnp.sum(norm, axis=0, keepdims=True), jnp.sum(cross, axis=0, keepdims=True),
                 jnp.zeros((6, G), F32)], axis=0))

        @pl.when(e == 0)
        def _():
            w = w2s[g]
            put(s + 2, w)
            send(exchange(s + 2))
            start = t32[:, cols]
            cur[g] = w
            w1s[g] = w
            reduce_start(start * start, w * start)

        @pl.when(e == 1)
        def _():
            total = ar_finish(s - 2, 0)
            norm, cross = total[0:1, :], total[1:2, :]
            step0 = norm / cross
            coef[g, 0:1, :] = norm
            coef[g, 1:2, :] = step0
            image = cur[g] - step0 * w2s[g]
            put(s + 2, image)
            send(exchange(s + 2))
            cur[g] = image
            res = t32[:, cols] - step0 * w1s[g]
            r1s[g] = res
            steps[g] = w2s[g]
            reduce_start(res * res, image * res)

        @pl.when(e == 2)
        def _():
            momentum, step1 = coef[g, 2:3, :], coef[g, 3:4, :]
            img_ref[:, cols] = cur[g] - step1 * (w2s[g] + momentum * steps[g])

        @pl.when((s >= 1) & (s <= 4))
        def _():
            ar_start(s - 1, 0, ar_finish(s - 1, 1))

        return 0

    lax.fori_loop(0, 6, step, 0)

    for i in range(8):
        f_copy(i).wait_send()
    for slot in (M1, P1, M2, P2):
        s_copy(slot).wait_send()

    def finish(s, _):
        drain(exchange(s))

        @pl.when(s < 4)
        def _():
            for axis in range(3):
                for copy in ar_copies(s, axis):
                    copy.wait_send()

        return 0

    lax.fori_loop(0, 6, finish, 0)


def body(features, targets, nugget, pattern):
    out = jax.ShapeDtypeStruct((T, 2 * G), F32)
    inputs = (features, targets, nugget.reshape(1, T), pattern)
    dma = pltpu.SemaphoreType.DMA
    return pl.pallas_call(
        kernel,
        out_shape=(out, out, out),
        in_specs=[
            pl.BlockSpec(memory_space=pl.ANY),
            pl.BlockSpec(memory_space=pl.ANY),
            pl.BlockSpec(memory_space=pltpu.VMEM),
            pl.BlockSpec(memory_space=pltpu.SMEM),
        ],
        out_specs=(pl.BlockSpec(memory_space=pltpu.VMEM),) * 3,
        scratch_shapes=[
            pltpu.VMEM((T, D), F32),
            pltpu.VMEM((T, 2 * G), F32),
            pltpu.VMEM((T, D), BF16),
            pltpu.VMEM((5, T, D), BF16),
            pltpu.VMEM((T, G), F32),
            pltpu.VMEM((T, 5 * T), BF16),
            pltpu.VMEM((T, G), F32),
            pltpu.VMEM((6, 10, H, G), BF16),
            pltpu.VMEM((6, 2, H, G), BF16),
            pltpu.VMEM((2, T, G), F32),
            pltpu.VMEM((2, T, G), F32),
            pltpu.VMEM((2, T, G), F32),
            pltpu.VMEM((2, T, G), F32),
            pltpu.VMEM((2, T, G), F32),
            pltpu.VMEM((2, 8, G), F32),
            pltpu.VMEM((4, X, 8, G), F32),
            pltpu.VMEM((4, Y, 8, G), F32),
            pltpu.VMEM((4, Z, 8, G), F32),
            dma((2,)),
            dma((8,)),
            dma((8,)),
            dma((5,)),
            dma((5,)),
            dma((6, 10)),
            dma((6, 10)),
            dma((4, X + Y + Z - 3)),
            dma((4, X + Y + Z - 3)),
        ],
        compiler_params=pltpu.CompilerParams(
            collective_id=0, has_side_effects=True, vmem_limit_bytes=46 * 2**20
        ),
        name="cascaded_cg",
    )(*(pltpu.with_memory_space_constraint(array, pltpu.HBM) for array in inputs))


def solution(mesh):
    return jax.shard_map(
        body,
        mesh=mesh,
        in_specs=(P("rows", None), P("rows", "out"), P("rows"), P("rows", None)),
        out_specs=(P("rows", "out"), P("rows", "out"), P("rows", "out")),
        check_vma=False,
    )
```
